512 devices in a mesh: dp: 16 (over y, core), expert: 8 (over z), tensor: 4 (over x).
Axes of the slice: x: 4, y: 8, z: 8, core: 2. Of those that a mesh axis runs over, the one named last changes fastest.
Arguments:
- queries: bfloat16 [8192, 4096], P(('dp', 'expert'), 'tensor'), may hold values from -6 to 6
- keys: bfloat16 [8192, 512], P(('dp', 'expert'), 'tensor'), may hold values from -6 to 6
- values: bfloat16 [8192, 512], P(('dp', 'expert'), 'tensor'), may hold values from -6 to 6
- image_start: int32 [16, 4], P('dp'), may hold values from 0 to 448, as said below
- norm_gain: bfloat16 [4096], P('tensor'), may hold values from 0.099609375 to 1.8984375
- expert_ids: int32 [8192, 8], P(('dp', 'expert')), may hold values from 0 to 127, all different within a row; in each aligned block of 64 rows (0 to 63, 64 to 127, ...) at most 8 rows name the same one
- gate_values: float32 [8192, 8], P(('dp', 'expert')), may hold values from 0.03 to 0.3
- gate_weight: bfloat16 [128, 4096, 768], P(('dp', 'expert'), 'tensor'), may hold values from -0.09375 to 0.09375
- up_weight: bfloat16 [128, 4096, 768], P(('dp', 'expert'), 'tensor'), may hold values from -0.09375 to 0.09375
- down_weight: bfloat16 [128, 768, 4096], P(('dp', 'expert'), None, 'tensor'), may hold values from -0.21875 to 0.21875
Outputs:
- mixed: bfloat16 [8192, 4096], P(('dp', 'expert'), 'tensor')
The draws below stay inside these ranges and needn't reach their ends.
Inputs may be any that keep to these rules, and one draw needn't show every extreme that they name: The images of a rollout are in order and disjoint; image k covers 64 positions from image_start and lies within positions 2 * k * 64 to 2 * (k + 1) * 64 - 1. `expert_ids`: among the rows of one device, no expert is named by more than 8 rows.
All inputs are finite; a program needn't handle non-finite values.
Results may differ from the reference program's by a relative error of at most 0.029.
Values may be sent and summed in bfloat16 or wider, within the bound.
No kernel may reach another device: no remote copies, remote signals or barrier semaphores. Data moves between devices by JAX's collectives and lax.ppermute only.
A program may use at most 64 MiB of HBM per device.

```python
import math
import jax
import jax.numpy as jnp
import numpy as np
from jax import lax

D = 4096
HD = 128
HQ = 32
KVH = 4
FF = 768
TOP = 8
TOK_DEV = 64
EXPERTS = 128
ROLLOUTS = 16
L = 512
TOKENS = 8192
NSPAN = 4
IMG = 64
CAP = 8
FEAT_DEV = 1024


def draw_queries(key, part):
    key = jax.random.fold_in(key, 1)
    result = jnp.clip(jax.random.normal(key, (TOKENS, HQ * HD)), -6.0, 6.0)
    return result.astype(jnp.bfloat16)


def draw_keys(key, part):
    key = jax.random.fold_in(key, 2)
    result = jnp.clip(jax.random.normal(key, (TOKENS, KVH * HD)), -6.0, 6.0)
    return result.astype(jnp.bfloat16)


def draw_image_start(key, part):
    key = jax.random.fold_in(key, 7)
    offsets = jax.random.randint(key, (ROLLOUTS, NSPAN), 0, TOK_DEV + 1)
    offsets = offsets.at[0, 0].set(0)
    offsets = offsets.at[ROLLOUTS - 1, NSPAN - 1].set(TOK_DEV)
    anchor = 2 * TOK_DEV * jnp.arange(NSPAN, dtype=jnp.int32)
    return (anchor[None, :] + offsets).astype(jnp.int32)


def level_of(stream_key, extent, cuts, least, high):
    factor_of, own = 1.0, jax.random.fold_in(stream_key, 6)
    for axis_at, parts in cuts:
        heights = jnp.exp(jax.random.uniform(jax.random.fold_in(own, axis_at), (parts,), jnp.float32, least / len(cuts), high / len(cuts)))
        factor_of = factor_of * jnp.repeat(heights, extent[axis_at] // parts).reshape([-1 if axis == axis_at else 1 for axis in range(len(extent))])
    return factor_of


def assign_block(key, own, number, rows, amount, top, reach, slope):
    sequence = jax.random.permutation(key, amount)
    crowded, common = shares(amount, rows * top, reach, slope, True), shares(amount, rows * top, reach, slope, False)
    places = jnp.arange(amount)

    def named(sizes, rotation):
        used = int((sizes > 0).sum())
        fixed = max(1, used // 4)
        shifted = fixed + (places - fixed + rotation * (used - fixed)) % max(1, amount - fixed)
        return jnp.zeros((amount,), jnp.int32).at[sequence[jnp.where(places < fixed, places, shifted)]].set(jnp.asarray(sizes, jnp.int32))

    sizes = jnp.where(number % 4 == 0, named(crowded, number // 4), named(common, number - number // 4 - 1))
    mixed = jax.random.permutation(jax.random.fold_in(own, 3), amount)
    donor, taker = mixed[0:amount // 2 * 2:2], mixed[1:amount // 2 * 2:2]
    margin = jnp.minimum(sizes[donor] - 1, reach - sizes[taker]) // 2
    margin = jnp.where((donor == sequence[0]) | (taker == sequence[0]) | (sizes[taker] == 0), 0, jnp.maximum(margin, 0))
    shifted = jax.random.randint(jax.random.fold_in(own, 4), (amount // 2,), 0, 1 << 20) % (margin + 1)
    sizes = sizes.at[donor].add(-shifted).at[taker].add(shifted)
    members = jnp.searchsorted(jnp.cumsum(sizes), jnp.arange(rows * top), side="right").astype(jnp.int32)
    grid = members.reshape(top, rows).T
    grid = grid[jax.random.permutation(jax.random.fold_in(own, 1), rows)]
    rotation = jax.random.randint(jax.random.fold_in(own, 2), (rows, 1), 0, top)
    return jnp.take_along_axis(grid, (jnp.arange(top)[None, :] + rotation) % top, axis=1)


def shares(number_of, total, reach, lean, full):
    weights = [(1 << 20) // math.isqrt(rank ** lean) + 1 for rank in range(1, number_of + 1)]
    largest = reach if full else min(reach, max(-(-total // number_of), total * weights[0] // sum(weights)))
    least = 1 if total - largest >= number_of - 1 else 0
    counts, rest = [largest] + [least] * (number_of - 1), total - largest - least * (number_of - 1)
    while rest > 0:
        movable = [i for i in range(1, number_of) if counts[i] < largest] or [i for i in range(1, number_of) if counts[i] < reach]
        mass, remaining = sum([weights[i] for i in movable]), rest
        for i in movable:
            extra = min(reach - counts[i], max(1, remaining * weights[i] // mass), rest)
            counts[i] = counts[i] + extra
            rest = rest - extra
    return np.array(counts)


def scatter_about(stream_key, dims, width, bound, pieces=(), kind=jnp.bfloat16):
    values = jax.random.normal(stream_key, dims, jnp.float32) * width
    if len(pieces) > 0:
        values = level_of(stream_key, dims, pieces, -0.22, 0.18) * values
    return jnp.clip(values, min=-bound, max=bound).astype(kind)


def setup_inputs(seed: int = 0) -> dict:
    splits = jax.random.split(jax.random.key(seed), 11)
    queries = draw_queries(jax.random.fold_in(splits[10], 71), 0)
    keys = draw_keys(jax.random.fold_in(splits[10], 71), 0)
    values = scatter_about(splits[2], (TOKENS, KVH * HD), 1.0, 6.0, ((0, 128), (1, 4)))
    image_start = draw_image_start(jax.random.fold_in(splits[10], 71), 0)
    norm_gain = jnp.clip(1.0 + 0.18 * jax.random.normal(splits[4], (D,), jnp.float32), 0.099609375, 1.8984375).astype(jnp.bfloat16)
    expert_ids_keys = jax.random.split(jax.random.fold_in(splits[5], 1), TOKENS // TOK_DEV)
    expert_ids_turns = jax.random.permutation(jax.random.fold_in(splits[5], 3), TOKENS // TOK_DEV)
    expert_ids = jax.vmap(lambda own, number: assign_block(jax.random.fold_in(splits[5], 2), own, number, TOK_DEV, EXPERTS, TOP, CAP, 2))(expert_ids_keys, expert_ids_turns).reshape((TOKENS, TOP))
    gate_values = jnp.clip(jnp.exp(math.log(0.3) - 2.3025852 * jax.random.uniform(splits[6], (TOKENS, TOP), jnp.float32) ** level_of(splits[6], (TOKENS, TOP), ((0, 128),), -0.2, 0.2)), 0.03, 0.3)
    gate_weight = scatter_about(splits[7], (EXPERTS, D, FF), D ** -0.5, 0.09375, ((0, 128), (1, 4)))
    up_weight = scatter_about(splits[8], (EXPERTS, D, FF), D ** -0.5, 0.09375, ((0, 128), (1, 4)))
    down_weight = scatter_about(splits[9], (EXPERTS, FF, D), FF ** -0.5, 0.21875, ((0, 128), (2, 4)))
    return {"queries": queries, "keys": keys, "values": values, "image_start": image_start, "norm_gain": norm_gain, "expert_ids": expert_ids, "gate_values": gate_values, "gate_weight": gate_weight, "up_weight": up_weight, "down_weight": down_weight}


def image_limits(positions, starts):
    inside = (positions[:, None] >= starts[None, :]) & (positions[:, None] < starts[None, :] + IMG)
    ends = jnp.broadcast_to(starts[None, :] + IMG - 1, inside.shape)
    return lax.optimization_barrier(jnp.max(jnp.where(inside, ends, positions[:, None]), axis=1))

def attend_rollout(operands):
    rollout_q, rollout_k, rollout_v, starts = operands
    positions = jnp.arange(L, dtype=jnp.int32)
    visible_end = image_limits(positions, starts.astype(jnp.int32))
    visible = positions[None, :] <= visible_end[:, None]
    group_size = HQ // KVH
    keys_wide = jnp.repeat(rollout_k, group_size, axis=1).astype(jnp.float32)
    values_wide = jnp.repeat(rollout_v, group_size, axis=1).astype(jnp.float32)
    score_scale = 1.0 / math.sqrt(HD)
    scores = jnp.einsum('qhd,khd->hqk', rollout_q.astype(jnp.float32), keys_wide) * score_scale
    masked = jnp.where(visible[None], scores, -1e+30)
    row_max = lax.optimization_barrier(jnp.max(masked, axis=2, keepdims=True))
    weights = jnp.where(visible[None], jnp.exp(scores - row_max), 0.0)
    row_total = lax.optimization_barrier(jnp.sum(weights, axis=2))
    rounded = lax.optimization_barrier(weights.astype(jnp.bfloat16)).astype(jnp.float32)
    summed = jnp.einsum('hqk,khd->hqd', rounded, values_wide)
    result = summed / row_total[:, :, None]
    return jnp.transpose(result, (1, 0, 2)).reshape(L, HQ * HD).astype(jnp.bfloat16)

def reference(queries, keys, values, image_start, norm_gain, expert_ids, gate_values, gate_weight, up_weight, down_weight):
    attended = lax.map(attend_rollout, (queries.reshape(ROLLOUTS, L, HQ, HD), keys.reshape(ROLLOUTS, L, KVH, HD), values.reshape(ROLLOUTS, L, KVH, HD), image_start))
    attended = attended.reshape(TOKENS, D)
    wide = attended.astype(jnp.float32)
    mean_square = lax.optimization_barrier(jnp.mean(wide * wide, axis=1, keepdims=True))
    normed = (wide * lax.rsqrt(mean_square + 1e-06) * norm_gain.astype(jnp.float32)).astype(jnp.bfloat16)
    flat_ids = expert_ids.reshape(-1)
    flat_gates = gate_values.reshape(-1)
    route_count = TOKENS * TOP

    def one_expert(expert_mix, operands):
        expert_index, gate_matrix, up_matrix, down_matrix = operands
        chosen = jnp.nonzero(flat_ids == expert_index, size=EXPERTS * CAP, fill_value=route_count)[0].astype(jnp.int32)
        valid = chosen < route_count
        safe_route = jnp.where(valid, chosen, 0).astype(jnp.int32)
        token_index = (safe_route // TOP).astype(jnp.int32)
        slot_rows = normed[token_index]
        gate_sum = jnp.zeros((EXPERTS * CAP, FF), jnp.float32)
        up_sum = jnp.zeros((EXPERTS * CAP, FF), jnp.float32)
        for block in range(D // FEAT_DEV):
            low = block * FEAT_DEV
            high = low + FEAT_DEV
            gate_part = jnp.dot(slot_rows[:, low:high], gate_matrix[low:high], preferred_element_type=jnp.float32)
            up_part = jnp.dot(slot_rows[:, low:high], up_matrix[low:high], preferred_element_type=jnp.float32)
            gate_sum = gate_sum + lax.optimization_barrier(gate_part.astype(jnp.bfloat16)).astype(jnp.float32)
            up_sum = up_sum + lax.optimization_barrier(up_part.astype(jnp.bfloat16)).astype(jnp.float32)
        hidden = (jax.nn.silu(gate_sum) * up_sum).astype(jnp.bfloat16)
        produced = jnp.dot(hidden, down_matrix, preferred_element_type=jnp.float32).astype(jnp.bfloat16)
        weight_here = jnp.where(valid, flat_gates[safe_route], 0.0)
        expert_mix = expert_mix.at[token_index].add(weight_here[:, None] * produced.astype(jnp.float32))
        return (expert_mix, None)
    initial = jnp.zeros((TOKENS, D), jnp.float32)
    expert_mix, unused = lax.scan(one_expert, initial, (jnp.arange(EXPERTS, dtype=jnp.int32), gate_weight, up_weight, down_weight))
    return (wide + expert_mix).astype(jnp.bfloat16)
```

```python
import functools
import math

import jax
import jax.numpy as jnp
from jax import lax
from jax.experimental import pallas as pl
from jax.experimental.pallas import tpu as pltpu
from jax.sharding import Mesh
from jax.sharding import PartitionSpec as P

D = 4096
CAP = 8
LANES = 128
BF = jnp.bfloat16
F32 = jnp.float32
GROUP = ("y", "expert")


def ring(size, step):
    return [(i, (i + step) % size) for i in range(size)]


def whole(shape):
    return pl.BlockSpec(shape, lambda *_: (0,) * len(shape))


def attention(queries, keys, values, image_start):
    tok_rows, head_size = keys.shape
    heads_here = queries.shape[1] // head_size
    blocks = lax.axis_size("expert")
    query_pos = lax.axis_index("expert") * tok_rows + jnp.arange(tok_rows, dtype=jnp.int32)
    starts = image_start[0]
    inside = (query_pos[:, None] >= starts[None, :]) & (
        query_pos[:, None] < starts[None, :] + tok_rows
    )
    ends = jnp.broadcast_to(starts[None, :] + tok_rows - 1, inside.shape)
    visible_end = jnp.max(jnp.where(inside, ends, query_pos[:, None]), axis=1)
    grouped = queries.reshape(tok_rows, heads_here, head_size)
    own = jnp.concatenate([keys, values], axis=1)
    copies = jnp.broadcast_to(own[None], (blocks,) + own.shape)
    both = lax.all_to_all(copies, "expert", split_axis=0, concat_axis=0, tiled=True)
    both = both.reshape(blocks * tok_rows, 2 * head_size)
    all_keys, all_values = both[:, :head_size], both[:, head_size:]
    scores = jnp.einsum("thd,nd->htn", grouped, all_keys, preferred_element_type=F32)
    scores = scores * (1.0 / math.sqrt(head_size))
    key_pos = jnp.arange(all_keys.shape[0], dtype=jnp.int32)
    visible = (key_pos[None, :] <= visible_end[:, None])[None]
    row_max = jnp.max(jnp.where(visible, scores, -1e30), axis=2, keepdims=True)
    weights = jnp.where(visible, jnp.exp(scores - row_max), 0.0)
    row_total = jnp.sum(weights, axis=2)
    summed = jnp.einsum("htn,nd->htd", weights.astype(BF), all_values, preferred_element_type=F32)
    result = summed / row_total[:, :, None]
    return jnp.transpose(result, (1, 0, 2)).reshape(tok_rows, heads_here * head_size).astype(BF)


def gate_up_kernel(here, rows, gain, gate, up, *rest, size, waits):
    outs, scaled = rest[waits : waits + size], rest[waits + size]
    block = rows.shape[0] // size
    hidden = gate.shape[1]
    step = pl.program_id(0)

    @pl.when(step == 0)
    def _():
        lane = lax.broadcasted_iota(jnp.int32, (block, LANES), 1)
        for k in range(size):
            at = lax.rem(here[0] + k, size) * block
            wide = rows[pl.ds(pl.multiple_of(at, block), block), :].astype(F32)
            squares = jnp.sum(wide * wide, axis=1, keepdims=True)
            high = squares.astype(BF).astype(F32)
            extra = jnp.where(lane == 0, high, jnp.where(lane == 1, squares - high, 0.0))
            outs[k][:, 2 * hidden :] = extra.astype(BF)
            scaled[pl.ds(k * block, block), :] = (wide * gain[...].astype(F32)).astype(BF)

    def product(weight, low):
        part = jnp.dot(scaled[...], weight[...], preferred_element_type=F32).astype(BF)
        for k in range(size):
            outs[k][:, low : low + hidden] = part[k * block : (k + 1) * block, :]

    @pl.when(step == 0)
    def _():
        product(gate, 0)

    @pl.when(step == 1)
    def _():
        product(up, hidden)


def gate_up(here, rows, gain, gate, up, after):
    size = lax.axis_size("tensor")
    feat, hidden = gate.shape
    block = rows.shape[0] // size
    width = 2 * hidden + LANES
    kernel = functools.partial(gate_up_kernel, size=size, waits=len(after))
    return pl.pallas_call(
        kernel,
        grid_spec=pltpu.PrefetchScalarGridSpec(
            num_scalar_prefetch=1,
            grid=(2,),
            in_specs=[whole(rows.shape), whole((1, feat)), whole(gate.shape), whole(up.shape)]
            + [pl.BlockSpec(memory_space=pl.ANY)] * len(after),
            out_specs=[whole((block, width))] * size,
            scratch_shapes=[pltpu.VMEM(rows.shape, BF)],
        ),
        out_shape=[jax.ShapeDtypeStruct((block, width), BF)] * size,
        compiler_params=pltpu.CompilerParams(vmem_limit_bytes=32 * 1024 * 1024),
        cost_estimate=pl.CostEstimate(
            flops=4 * rows.shape[0] * feat * hidden,
            bytes_accessed=2 * (rows.size + 2 * gate.size + rows.shape[0] * width),
            transcendentals=0,
        ),
    )(here, rows, gain, gate, up, *after)


def down_kernel(here, *refs, size, waits):
    pieces, down = refs[:size], refs[size]
    made, hidden = refs[size + 1 + waits], refs[size + 2 + waits]
    block = pieces[0].shape[0]

    @pl.when(pl.program_id(0) == 0)
    def _():
        for k in range(size):
            at = lax.rem(here[0] + size - k, size) * block
            hidden[pl.ds(pl.multiple_of(at, block), block), :] = pieces[k][...]

    made[...] = jnp.dot(hidden[...], down[...], preferred_element_type=F32).astype(BF)


def down_product(here, pieces, down, after):
    size = len(pieces)
    block, hidden = pieces[0].shape
    feat = down.shape[1]
    half = feat // 2
    rows = size * block
    return pl.pallas_call(
        functools.partial(down_kernel, size=size, waits=len(after)),
        grid_spec=pltpu.PrefetchScalarGridSpec(
            num_scalar_prefetch=1,
            grid=(2,),
            in_specs=[whole((block, hidden))] * size
            + [pl.BlockSpec((hidden, half), lambda i, _: (0, i))]
            + [pl.BlockSpec(memory_space=pl.ANY)] * len(after),
            out_specs=pl.BlockSpec((rows, half), lambda i, _: (0, i)),
            scratch_shapes=[pltpu.VMEM((rows, hidden), BF)],
        ),
        out_shape=jax.ShapeDtypeStruct((rows, feat), BF),
        compiler_params=pltpu.CompilerParams(vmem_limit_bytes=32 * 1024 * 1024),
        cost_estimate=pl.CostEstimate(
            flops=2 * rows * hidden * feat,
            bytes_accessed=2 * (rows * hidden + hidden * feat + rows * feat),
            transcendentals=0,
        ),
    )(here, *pieces, down, *after)


def silu_product(parts, hidden):
    total = parts[0].astype(F32)
    for part in parts[1:]:
        total = total + part.astype(F32)
    squares = total[:, 2 * hidden : 2 * hidden + 1] + total[:, 2 * hidden + 1 : 2 * hidden + 2]
    scale = lax.rsqrt(squares / D + 1e-06)
    gate_sum = total[:, :hidden] * scale
    up_sum = total[:, hidden : 2 * hidden] * scale
    return (jax.nn.silu(gate_sum) * up_sum).astype(BF)


def exchange(block):
    return lax.all_to_all(block, GROUP, split_axis=0, concat_axis=0, tiled=True)


def swap(block):
    return lax.ppermute(block, "core", [(0, 1), (1, 0)])


def per_device(
    queries,
    keys,
    values,
    image_start,
    norm_gain,
    expert_ids,
    gate_values,
    gate_weight,
    up_weight,
    down_weight,
):
    tok_rows, feat = queries.shape
    hidden_size = gate_weight.shape[2]
    size = lax.axis_size("tensor")
    zs = lax.axis_size("expert")
    peers = lax.axis_size("y") * zs
    rows = peers * CAP
    core = lax.axis_index("core")
    here = lax.axis_index("tensor").astype(jnp.int32)[None]
    gain = norm_gain[None]
    gate_rows, up_rows, down_rows = gate_weight[0], up_weight[0], down_weight[0]

    token = jnp.arange(tok_rows, dtype=jnp.int32)
    earlier = (token[:, None] < token[None, :]).astype(BF)
    level = jnp.arange(CAP, dtype=jnp.int32)[None, :, None]
    peer = jnp.arange(peers, dtype=jnp.int32)

    def plan(side):
        experts = (peer // zs * 2 + side) * zs + peer % zs
        named = expert_ids.T[:, None, :] == experts[None, :, None]
        member = jnp.any(named, axis=0)
        gate_of = jnp.sum(jnp.where(named, gate_values.T[:, None, :], 0.0), axis=0)
        rank = jnp.dot(member.astype(BF), earlier, preferred_element_type=F32)
        place = jnp.where(member, rank.astype(jnp.int32), -1)
        hit = place[:, None, :] == level
        high = lax.reduce_precision(gate_of, 8, 7)
        gates = jnp.concatenate([high, gate_of - high], axis=1)
        mix = jnp.where(jnp.concatenate([hit, hit], axis=2), gates[:, None, :], 0.0)
        pick = hit.astype(BF).reshape(rows, tok_rows)
        return pick, mix.astype(BF).reshape(rows, 2 * tok_rows)

    pick_near, mix_near = plan(core)
    pick_far, mix_far = plan(1 - core)
    attended = attention(queries, keys, values, image_start)

    def outgoing(pick):
        return jnp.dot(pick, attended, preferred_element_type=F32).astype(BF)

    def blocks(flat):
        return flat.reshape(peers, CAP, feat)

    def reduce_parts(parts):
        got = [parts[0]]
        for step in range(1, size):
            got.append(lax.ppermute(parts[step], "tensor", ring(size, step)))
        return silu_product(got, hidden_size)

    def spread(piece):
        return [piece] + [lax.ppermute(piece, "tensor", ring(size, k)) for k in range(1, size)]

    def combine(mix, returned):
        both = lax.dot_general(
            mix,
            returned.reshape(rows, feat),
            (((0,), (0,)), ((), ())),
            preferred_element_type=F32,
        )
        return both[:tok_rows] + both[tok_rows:]

    near = exchange(blocks(outgoing(pick_near))).reshape(rows, feat)
    far = exchange(blocks(swap(outgoing(pick_far)))).reshape(rows, feat)

    near_parts = gate_up(here, near, gain, gate_rows, up_rows, [])
    near_hidden = reduce_parts(near_parts)
    far_parts = gate_up(here, far, gain, gate_rows, up_rows, [near_hidden])
    near_made = down_product(here, spread(near_hidden), down_rows, [far_parts[0]])
    near_back = exchange(blocks(near_made))
    far_hidden = reduce_parts(far_parts)
    far_made = down_product(here, spread(far_hidden), down_rows, [])
    far_back = exchange(blocks(swap(far_made)))

    mixed = attended.astype(F32) + combine(mix_near, near_back) + combine(mix_far, far_back)
    return mixed.astype(BF)


def solution(mesh):
    dp, expert, tensor = mesh.devices.shape
    split = Mesh(
        mesh.devices.reshape(dp // 2, 2, expert, tensor), ("y", "core", "expert", "tensor")
    )
    both = ("y", "core", "expert")
    return jax.shard_map(
        per_device,
        mesh=split,
        in_specs=(
            P(both, "tensor"),
            P(both, "tensor"),
            P(both, "tensor"),
            P(("y", "core"), None),
            P("tensor"),
            P(both, None),
            P(both, None),
            P(both, "tensor", None),
            P(both, "tensor", None),
            P(both, None, "tensor"),
        ),
        out_specs=P(both, "tensor"),
        check_vma=False,
    )
```

```python
import functools
import math

import jax
import jax.numpy as jnp
from jax import lax
from jax.experimental import pallas as pl
from jax.experimental.pallas import tpu as pltpu
from jax.sharding import Mesh
from jax.sharding import PartitionSpec as P

D = 4096
CAP = 8
LANES = 128
VMEM_LIMIT = 32 * 1024 * 1024
BF = jnp.bfloat16
F32 = jnp.float32
GROUP = ("y", "expert")


def ring(size, step):
    return [(i, (i + step) % size) for i in range(size)]


def whole(shape):
    return pl.BlockSpec(shape, lambda *_: (0,) * len(shape))


def attention(queries, keys, values, image_start):
    tok_rows, head_size = keys.shape
    heads_here = queries.shape[1] // head_size
    blocks = lax.axis_size("expert")
    query_pos = lax.axis_index("expert") * tok_rows + jnp.arange(tok_rows, dtype=jnp.int32)
    starts = image_start[0]
    inside = (query_pos[:, None] >= starts[None, :]) & (
        query_pos[:, None] < starts[None, :] + tok_rows
    )
    ends = jnp.broadcast_to(starts[None, :] + tok_rows - 1, inside.shape)
    visible_end = jnp.max(jnp.where(inside, ends, query_pos[:, None]), axis=1)
    grouped = queries.reshape(tok_rows, heads_here, head_size)
    own = jnp.concatenate([keys, values], axis=1)
    copies = jnp.broadcast_to(own[None], (blocks,) + own.shape)
    both = lax.all_to_all(copies, "expert", split_axis=0, concat_axis=0, tiled=True)
    both = both.reshape(blocks * tok_rows, 2 * head_size)
    all_keys, all_values = both[:, :head_size], both[:, head_size:]
    scores = jnp.einsum("thd,nd->htn", grouped, all_keys, preferred_element_type=F32)
    scores = scores * (1.0 / math.sqrt(head_size))
    key_pos = jnp.arange(all_keys.shape[0], dtype=jnp.int32)
    visible = (key_pos[None, :] <= visible_end[:, None])[None]
    row_max = jnp.max(jnp.where(visible, scores, -1e30), axis=2, keepdims=True)
    weights = jnp.where(visible, jnp.exp(scores - row_max), 0.0)
    row_total = jnp.sum(weights, axis=2)
    summed = jnp.einsum("htn,nd->htd", weights.astype(BF), all_values, preferred_element_type=F32)
    result = summed / row_total[:, :, None]
    return jnp.transpose(result, (1, 0, 2)).reshape(tok_rows, heads_here * head_size).astype(BF)


def gate_up_kernel(here, rows, gain, gate, up, *rest, size, waits):
    outs, scaled = rest[waits : waits + size], rest[waits + size]
    block = rows.shape[0] // size
    hidden = gate.shape[1]
    step = pl.program_id(0)

    @pl.when(step == 0)
    def _():
        lane = lax.broadcasted_iota(jnp.int32, (block, LANES), 1)
        for k in range(size):
            at = lax.rem(here[0] + k, size) * block
            wide = rows[pl.ds(pl.multiple_of(at, block), block), :].astype(F32)
            squares = jnp.sum(wide * wide, axis=1, keepdims=True)
            high = squares.astype(BF).astype(F32)
            extra = jnp.where(lane == 0, high, jnp.where(lane == 1, squares - high, 0.0))
            outs[k][:, 2 * hidden :] = extra.astype(BF)
            scaled[pl.ds(k * block, block), :] = (wide * gain[...].astype(F32)).astype(BF)

    def product(weight, low):
        part = jnp.dot(scaled[...], weight[...], preferred_element_type=F32).astype(BF)
        for k in range(size):
            outs[k][:, low : low + hidden] = part[k * block : (k + 1) * block, :]

    @pl.when(step == 0)
    def _():
        product(gate, 0)

    @pl.when(step == 1)
    def _():
        product(up, hidden)


def gate_up(here, rows, gain, gate, up, after):
    size = lax.axis_size("tensor")
    feat, hidden = gate.shape
    block = rows.shape[0] // size
    width = 2 * hidden + LANES
    kernel = functools.partial(gate_up_kernel, size=size, waits=len(after))
    return pl.pallas_call(
        kernel,
        grid_spec=pltpu.PrefetchScalarGridSpec(
            num_scalar_prefetch=1,
            grid=(2,),
            in_specs=[whole(rows.shape), whole((1, feat)), whole(gate.shape), whole(up.shape)]
            + [pl.BlockSpec(memory_space=pl.ANY)] * len(after),
            out_specs=[whole((block, width))] * size,
            scratch_shapes=[pltpu.VMEM(rows.shape, BF)],
        ),
        out_shape=[jax.ShapeDtypeStruct((block, width), BF)] * size,
        compiler_params=pltpu.CompilerParams(vmem_limit_bytes=VMEM_LIMIT),
        cost_estimate=pl.CostEstimate(
            flops=4 * rows.shape[0] * feat * hidden,
            bytes_accessed=2 * (rows.size + 2 * gate.size + rows.shape[0] * width),
            transcendentals=0,
        ),
    )(here, rows, gain, gate, up, *after)


def down_kernel(here, *refs, size, waits):
    pieces, down = refs[:size], refs[size]
    made, hidden = refs[size + 1 + waits], refs[size + 2 + waits]
    block = pieces[0].shape[0]

    @pl.when(pl.program_id(0) == 0)
    def _():
        for k in range(size):
            at = lax.rem(here[0] + size - k, size) * block
            hidden[pl.ds(pl.multiple_of(at, block), block), :] = pieces[k][...]

    made[...] = jnp.dot(hidden[...], down[...], preferred_element_type=F32).astype(BF)


def down_product(here, pieces, down, after):
    size = len(pieces)
    block, hidden = pieces[0].shape
    feat = down.shape[1]
    half = feat // 2
    rows = size * block
    return pl.pallas_call(
        functools.partial(down_kernel, size=size, waits=len(after)),
        grid_spec=pltpu.PrefetchScalarGridSpec(
            num_scalar_prefetch=1,
            grid=(2,),
            in_specs=[whole((block, hidden))] * size
            + [pl.BlockSpec((hidden, half), lambda i, _: (0, i))]
            + [pl.BlockSpec(memory_space=pl.ANY)] * len(after),
            out_specs=pl.BlockSpec((rows, half), lambda i, _: (0, i)),
            scratch_shapes=[pltpu.VMEM((rows, hidden), BF)],
        ),
        out_shape=jax.ShapeDtypeStruct((rows, feat), BF),
        compiler_params=pltpu.CompilerParams(vmem_limit_bytes=VMEM_LIMIT),
        cost_estimate=pl.CostEstimate(
            flops=2 * rows * hidden * feat,
            bytes_accessed=2 * (rows * hidden + hidden * feat + rows * feat),
            transcendentals=0,
        ),
    )(here, *pieces, down, *after)


def silu_product(parts, hidden):
    total = parts[0].astype(F32)
    for part in parts[1:]:
        total = total + part.astype(F32)
    squares = total[:, 2 * hidden : 2 * hidden + 1] + total[:, 2 * hidden + 1 : 2 * hidden + 2]
    scale = lax.rsqrt(squares / D + 1e-06)
    gate_sum = total[:, :hidden] * scale
    up_sum = total[:, hidden : 2 * hidden] * scale
    return (jax.nn.silu(gate_sum) * up_sum).astype(BF)


def silu_kernel(*refs):
    parts, out = refs[:-1], refs[-1]
    hidden = out.shape[1]

    def total(low, width):
        result = parts[0][:, low : low + width].astype(F32)
        for part in parts[1:]:
            result = result + part[:, low : low + width].astype(F32)
        return result

    extra = total(2 * hidden, LANES)
    scale = lax.rsqrt((extra[:, :1] + extra[:, 1:2]) / D + 1e-06)
    gate_sum = total(0, hidden) * scale
    up_sum = total(hidden, hidden) * scale
    out[...] = (gate_sum / (1.0 + jnp.exp(-gate_sum)) * up_sum).astype(BF)


def silu_call(parts, hidden):
    rows = parts[0].shape[0]
    near = pl.BlockSpec(memory_space=pltpu.VMEM)
    return pl.pallas_call(
        silu_kernel,
        in_specs=[near] * len(parts),
        out_specs=near,
        out_shape=jax.ShapeDtypeStruct((rows, hidden), BF),
        compiler_params=pltpu.CompilerParams(vmem_limit_bytes=VMEM_LIMIT),
        cost_estimate=pl.CostEstimate(
            flops=16 * rows * hidden,
            bytes_accessed=2 * rows * hidden * (2 * len(parts) + 1),
            transcendentals=rows * hidden,
        ),
    )(*parts)


def exchange(block):
    return lax.all_to_all(block, GROUP, split_axis=0, concat_axis=0, tiled=True)


def swap(block):
    return lax.ppermute(block, "core", [(0, 1), (1, 0)])


def per_device(
    queries,
    keys,
    values,
    image_start,
    norm_gain,
    expert_ids,
    gate_values,
    gate_weight,
    up_weight,
    down_weight,
):
    tok_rows, feat = queries.shape
    hidden_size = gate_weight.shape[2]
    size = lax.axis_size("tensor")
    zs = lax.axis_size("expert")
    peers = lax.axis_size("y") * zs
    rows = peers * CAP
    core = lax.axis_index("core")
    here = lax.axis_index("tensor").astype(jnp.int32)[None]
    gain = norm_gain[None]
    gate_rows, up_rows, down_rows = gate_weight[0], up_weight[0], down_weight[0]

    token = jnp.arange(tok_rows, dtype=jnp.int32)
    earlier = (token[:, None] < token[None, :]).astype(BF)
    level = jnp.arange(CAP, dtype=jnp.int32)[None, :, None]
    peer = jnp.arange(peers, dtype=jnp.int32)

    def plan(side):
        experts = (peer // zs * 2 + side) * zs + peer % zs
        named = expert_ids.T[:, None, :] == experts[None, :, None]
        member = jnp.any(named, axis=0)
        gate_of = jnp.sum(jnp.where(named, gate_values.T[:, None, :], 0.0), axis=0)
        rank = jnp.dot(member.astype(BF), earlier, preferred_element_type=F32)
        place = jnp.where(member, rank.astype(jnp.int32), -1)
        hit = place[:, None, :] == level
        high = lax.reduce_precision(gate_of, 8, 7)
        gates = jnp.concatenate([high, gate_of - high], axis=1)
        mix = jnp.where(jnp.concatenate([hit, hit], axis=2), gates[:, None, :], 0.0)
        pick = hit.astype(BF).reshape(rows, tok_rows)
        return pick, mix.astype(BF).reshape(rows, 2 * tok_rows)

    pick_near, mix_near = plan(core)
    pick_far, mix_far = plan(1 - core)
    attended = attention(queries, keys, values, image_start)

    def outgoing(pick):
        return jnp.dot(pick, attended, preferred_element_type=F32).astype(BF)

    def blocks(flat):
        return flat.reshape(peers, CAP, feat)

    def fetch_parts(parts):
        return [parts[0]] + [
            lax.ppermute(parts[step], "tensor", ring(size, step)) for step in range(1, size)
        ]

    def spread(piece):
        return [piece] + [lax.ppermute(piece, "tensor", ring(size, k)) for k in range(1, size)]

    def combine(mix, returned):
        both = lax.dot_general(
            mix,
            returned.reshape(rows, feat),
            (((0,), (0,)), ((), ())),
            preferred_element_type=F32,
        )
        return both[:tok_rows] + both[tok_rows:]

    near = exchange(blocks(outgoing(pick_near))).reshape(rows, feat)
    far = exchange(blocks(swap(outgoing(pick_far)))).reshape(rows, feat)

    near_parts = gate_up(here, near, gain, gate_rows, up_rows, [])
    near_got = fetch_parts(near_parts)
    far_parts = gate_up(here, far, gain, gate_rows, up_rows, [near_got[size // 2]])
    near_got, far_parts = lax.optimization_barrier((near_got, far_parts))
    far_parts = list(far_parts)
    near_pieces = spread(silu_call(near_got, hidden_size))
    for step in range(1, size):
        near_pieces[step], far_parts[step] = lax.optimization_barrier(
            (near_pieces[step], far_parts[step])
        )
    near_made = down_product(here, near_pieces, down_rows, [far_parts[0]])
    far_got = fetch_parts(far_parts)
    near_back = exchange(blocks(near_made))
    far_pieces = spread(silu_product(far_got, hidden_size))
    far_made = down_product(here, far_pieces, down_rows, [])
    far_back = exchange(blocks(swap(far_made)))

    mixed = attended.astype(F32) + combine(mix_near, near_back) + combine(mix_far, far_back)
    return mixed.astype(BF)


def solution(mesh):
    dp, expert, tensor = mesh.devices.shape
    split = Mesh(
        mesh.devices.reshape(dp // 2, 2, expert, tensor), ("y", "core", "expert", "tensor")
    )
    both = ("y", "core", "expert")
    return jax.shard_map(
        per_device,
        mesh=split,
        in_specs=(
            P(both, "tensor"),
            P(both, "tensor"),
            P(both, "tensor"),
            P(("y", "core"), None),
            P("tensor"),
            P(both, None),
            P(both, None),
            P(both, "tensor", None),
            P(both, "tensor", None),
            P(both, None, "tensor"),
        ),
        out_specs=P(both, "tensor"),
        check_vma=False,
    )
```

```python
import functools
import math

import jax
import jax.numpy as jnp
from jax import lax
from jax.experimental import pallas as pl
from jax.experimental.pallas import tpu as pltpu
from jax.sharding import Mesh
from jax.sharding import PartitionSpec as P

D = 4096
CAP = 8
LANES = 128
VMEM_LIMIT = 32 * 1024 * 1024
WIDE_LIMIT = 50 * 1024 * 1024
BF = jnp.bfloat16
F32 = jnp.float32
GROUP = ("y", "expert")


def ring(size, step):
    return [(i, (i + step) % size) for i in range(size)]


def whole(shape):
    return pl.BlockSpec(shape, lambda *_: (0,) * len(shape))


def attention(queries, keys, values, image_start):
    tok_rows, head_size = keys.shape
    heads_here = queries.shape[1] // head_size
    blocks = lax.axis_size("expert")
    query_pos = lax.axis_index("expert") * tok_rows + jnp.arange(tok_rows, dtype=jnp.int32)
    starts = image_start[0]
    inside = (query_pos[:, None] >= starts[None, :]) & (
        query_pos[:, None] < starts[None, :] + tok_rows
    )
    ends = jnp.broadcast_to(starts[None, :] + tok_rows - 1, inside.shape)
    visible_end = jnp.max(jnp.where(inside, ends, query_pos[:, None]), axis=1)
    grouped = queries.reshape(tok_rows, heads_here, head_size)
    own = jnp.concatenate([keys, values], axis=1)
    copies = jnp.broadcast_to(own[None], (blocks,) + own.shape)
    both = lax.all_to_all(copies, "expert", split_axis=0, concat_axis=0, tiled=True)
    both = both.reshape(blocks * tok_rows, 2 * head_size)
    all_keys, all_values = both[:, :head_size], both[:, head_size:]
    scores = jnp.einsum("thd,nd->htn", grouped, all_keys, preferred_element_type=F32)
    scores = scores * (1.0 / math.sqrt(head_size))
    key_pos = jnp.arange(all_keys.shape[0], dtype=jnp.int32)
    visible = (key_pos[None, :] <= visible_end[:, None])[None]
    row_max = jnp.max(jnp.where(visible, scores, -1e30), axis=2, keepdims=True)
    weights = jnp.where(visible, jnp.exp(scores - row_max), 0.0)
    row_total = jnp.sum(weights, axis=2)
    summed = jnp.einsum("htn,nd->htd", weights.astype(BF), all_values, preferred_element_type=F32)
    result = summed / row_total[:, :, None]
    return jnp.transpose(result, (1, 0, 2)).reshape(tok_rows, heads_here * head_size).astype(BF)


def move(source, target, sem):
    copy = pltpu.make_async_copy(source, target, sem)
    copy.start()
    return copy


def gate_up_kernel(here, rows, gain, gate, up, *rest, size, waits):
    outs = rest[waits : waits + size]
    scaled, gate_held, up_held, sems = rest[waits + size :]
    count, feat = rows.shape
    hidden = gate.shape[1]
    block, slab = count // size, feat // size
    copies = []
    for source, target in ((gate, gate_held), (up, up_held)):
        for k in range(size):
            part = pl.ds(k * slab, slab)
            copies.append(move(source.at[part, :], target.at[part, :], sems.at[len(copies)]))

    lane = lax.broadcasted_iota(jnp.int32, (block, LANES), 1)
    for k in range(size):
        at = pl.multiple_of(lax.rem(here[0] + k, size) * block, block)
        wide = rows[pl.ds(at, block), :].astype(F32)
        squares = jnp.sum(wide * wide, axis=1, keepdims=True)
        high = squares.astype(BF).astype(F32)
        extra = jnp.where(lane == 0, high, jnp.where(lane == 1, squares - high, 0.0))
        outs[k][:, 2 * hidden :] = extra.astype(BF)
        scaled[k * block : (k + 1) * block, :] = (wide * gain[...].astype(F32)).astype(BF)

    def product(weight, low):
        part = jnp.dot(scaled[...], weight[...], preferred_element_type=F32).astype(BF)
        for k in range(size):
            outs[k][:, low : low + hidden] = part[k * block : (k + 1) * block, :]

    for copy in copies[:size]:
        copy.wait()
    product(gate_held, 0)
    for copy in copies[size:]:
        copy.wait()
    product(up_held, hidden)


def gate_up(here, rows, gain, gate, up, after):
    size = lax.axis_size("tensor")
    feat, hidden = gate.shape
    count = rows.shape[0]
    block = count // size
    width = 2 * hidden + LANES
    near, far = pl.BlockSpec(memory_space=pltpu.VMEM), pl.BlockSpec(memory_space=pl.ANY)
    return pl.pallas_call(
        functools.partial(gate_up_kernel, size=size, waits=len(after)),
        in_specs=[pl.BlockSpec(memory_space=pltpu.SMEM), near, near, far, far]
        + [pl.BlockSpec(memory_space=pl.ANY)] * len(after),
        out_specs=[near] * size,
        scratch_shapes=[
            pltpu.VMEM(rows.shape, BF),
            pltpu.VMEM(gate.shape, BF),
            pltpu.VMEM(up.shape, BF),
            pltpu.SemaphoreType.DMA((2 * size,)),
        ],
        out_shape=[jax.ShapeDtypeStruct((block, width), BF)] * size,
        compiler_params=pltpu.CompilerParams(vmem_limit_bytes=WIDE_LIMIT),
        cost_estimate=pl.CostEstimate(
            flops=4 * count * feat * hidden,
            bytes_accessed=2 * (rows.size + 2 * gate.size + count * width),
            transcendentals=0,
        ),
    )(here, rows, gain, gate, up, *after)


def down_kernel(here, *refs, size, waits):
    pieces, down = refs[:size], refs[size]
    made, hidden = refs[size + 1 + waits], refs[size + 2 + waits]
    block = pieces[0].shape[0]

    @pl.when(pl.program_id(0) == 0)
    def _():
        for k in range(size):
            at = lax.rem(here[0] + size - k, size) * block
            hidden[pl.ds(pl.multiple_of(at, block), block), :] = pieces[k][...]

    made[...] = jnp.dot(hidden[...], down[...], preferred_element_type=F32).astype(BF)


def down_product(here, pieces, down, after):
    size = len(pieces)
    block, hidden = pieces[0].shape
    feat = down.shape[1]
    half = feat // 2
    rows = size * block
    return pl.pallas_call(
        functools.partial(down_kernel, size=size, waits=len(after)),
        grid_spec=pltpu.PrefetchScalarGridSpec(
            num_scalar_prefetch=1,
            grid=(2,),
            in_specs=[whole((block, hidden))] * size
            + [pl.BlockSpec((hidden, half), lambda i, _: (0, i))]
            + [pl.BlockSpec(memory_space=pl.ANY)] * len(after),
            out_specs=pl.BlockSpec((rows, half), lambda i, _: (0, i)),
            scratch_shapes=[pltpu.VMEM((rows, hidden), BF)],
        ),
        out_shape=jax.ShapeDtypeStruct((rows, feat), BF),
        compiler_params=pltpu.CompilerParams(vmem_limit_bytes=VMEM_LIMIT),
        cost_estimate=pl.CostEstimate(
            flops=2 * rows * hidden * feat,
            bytes_accessed=2 * (rows * hidden + hidden * feat + rows * feat),
            transcendentals=0,
        ),
    )(here, *pieces, down, *after)


def silu_product(parts, hidden):
    total = parts[0].astype(F32)
    for part in parts[1:]:
        total = total + part.astype(F32)
    squares = total[:, 2 * hidden : 2 * hidden + 1] + total[:, 2 * hidden + 1 : 2 * hidden + 2]
    scale = lax.rsqrt(squares / D + 1e-06)
    gate_sum = total[:, :hidden] * scale
    up_sum = total[:, hidden : 2 * hidden] * scale
    return (jax.nn.silu(gate_sum) * up_sum).astype(BF)


def silu_kernel(*refs):
    parts, out = refs[:-1], refs[-1]
    hidden = out.shape[1]

    def total(low, width):
        result = parts[0][:, low : low + width].astype(F32)
        for part in parts[1:]:
            result = result + part[:, low : low + width].astype(F32)
        return result

    extra = total(2 * hidden, LANES)
    scale = lax.rsqrt((extra[:, :1] + extra[:, 1:2]) / D + 1e-06)
    gate_sum = total(0, hidden) * scale
    up_sum = total(hidden, hidden) * scale
    out[...] = (gate_sum / (1.0 + jnp.exp(-gate_sum)) * up_sum).astype(BF)


def silu_call(parts, hidden):
    rows = parts[0].shape[0]
    near = pl.BlockSpec(memory_space=pltpu.VMEM)
    return pl.pallas_call(
        silu_kernel,
        in_specs=[near] * len(parts),
        out_specs=near,
        out_shape=jax.ShapeDtypeStruct((rows, hidden), BF),
        compiler_params=pltpu.CompilerParams(vmem_limit_bytes=VMEM_LIMIT),
        cost_estimate=pl.CostEstimate(
            flops=16 * rows * hidden,
            bytes_accessed=2 * rows * hidden * (2 * len(parts) + 1),
            transcendentals=rows * hidden,
        ),
    )(*parts)


def exchange(block):
    return lax.all_to_all(block, GROUP, split_axis=0, concat_axis=0, tiled=True)


def swap(block):
    return lax.ppermute(block, "core", [(0, 1), (1, 0)])


def per_device(
    queries,
    keys,
    values,
    image_start,
    norm_gain,
    expert_ids,
    gate_values,
    gate_weight,
    up_weight,
    down_weight,
):
    tok_rows, feat = queries.shape
    hidden_size = gate_weight.shape[2]
    size = lax.axis_size("tensor")
    zs = lax.axis_size("expert")
    peers = lax.axis_size("y") * zs
    rows = peers * CAP
    core = lax.axis_index("core")
    here = lax.axis_index("tensor").astype(jnp.int32)[None]
    gain = norm_gain[None]
    gate_rows, up_rows, down_rows = gate_weight[0], up_weight[0], down_weight[0]

    token = jnp.arange(tok_rows, dtype=jnp.int32)
    earlier = (token[:, None] < token[None, :]).astype(BF)
    level = jnp.arange(CAP, dtype=jnp.int32)[None, :, None]
    peer = jnp.arange(peers, dtype=jnp.int32)

    def plan(side):
        experts = (peer // zs * 2 + side) * zs + peer % zs
        named = expert_ids.T[:, None, :] == experts[None, :, None]
        member = jnp.any(named, axis=0)
        gate_of = jnp.sum(jnp.where(named, gate_values.T[:, None, :], 0.0), axis=0)
        rank = jnp.dot(member.astype(BF), earlier, preferred_element_type=F32)
        place = jnp.where(member, rank.astype(jnp.int32), -1)
        hit = place[:, None, :] == level
        high = lax.reduce_precision(gate_of, 8, 7)
        gates = jnp.concatenate([high, gate_of - high], axis=1)
        mix = jnp.where(jnp.concatenate([hit, hit], axis=2), gates[:, None, :], 0.0)
        pick = hit.astype(BF).reshape(rows, tok_rows)
        return pick, mix.astype(BF).reshape(rows, 2 * tok_rows)

    pick_near, mix_near = plan(core)
    pick_far, mix_far = plan(1 - core)
    attended = attention(queries, keys, values, image_start)

    def outgoing(pick):
        return jnp.dot(pick, attended, preferred_element_type=F32).astype(BF)

    def blocks(flat):
        return flat.reshape(peers, CAP, feat)

    steps = sorted(range(1, size), key=lambda step: -min(step, size - step))

    def fetch_parts(parts):
        got = {step: lax.ppermute(parts[step], "tensor", ring(size, step)) for step in steps}
        return [parts[0]] + [got[step] for step in range(1, size)]

    def spread(piece):
        return fetch_parts([piece] * size)

    def combine(mix, returned):
        both = lax.dot_general(
            mix,
            returned.reshape(rows, feat),
            (((0,), (0,)), ((), ())),
            preferred_element_type=F32,
        )
        return both[:tok_rows] + both[tok_rows:]

    near = exchange(blocks(outgoing(pick_near))).reshape(rows, feat)
    far = exchange(blocks(swap(outgoing(pick_far)))).reshape(rows, feat)

    near_parts = gate_up(here, near, gain, gate_rows, up_rows, [])
    near_got = fetch_parts(near_parts)
    early = near_got[0].astype(F32) + near_got.pop(size // 2).astype(F32)
    near_pieces = spread(silu_call([early] + near_got[1:], hidden_size))
    far_parts = list(gate_up(here, far, gain, gate_rows, up_rows, [near_pieces[0]]))
    for step in steps:
        near_pieces[step], far_parts[step] = lax.optimization_barrier(
            (near_pieces[step], far_parts[step])
        )
    near_made = down_product(here, near_pieces, down_rows, [far_parts[0]])
    far_got = fetch_parts(far_parts)
    near_back = exchange(blocks(near_made))
    far_pieces = spread(silu_product(far_got, hidden_size))
    far_made = down_product(here, far_pieces, down_rows, [])
    far_back = exchange(blocks(swap(far_made)))

    mixed = attended.astype(F32) + combine(mix_near, near_back) + combine(mix_far, far_back)
    return mixed.astype(BF)


def solution(mesh):
    dp, expert, tensor = mesh.devices.shape
    split = Mesh(
        mesh.devices.reshape(dp // 2, 2, expert, tensor), ("y", "core", "expert", "tensor")
    )
    both = ("y", "core", "expert")
    return jax.shard_map(
        per_device,
        mesh=split,
        in_specs=(
            P(both, "tensor"),
            P(both, "tensor"),
            P(both, "tensor"),
            P(("y", "core"), None),
            P("tensor"),
            P(both, None),
            P(both, None),
            P(both, "tensor", None),
            P(both, "tensor", None),
            P(both, None, "tensor"),
        ),
        out_specs=P(both, "tensor"),
        check_vma=False,
    )
```

```python
import functools
import math

import jax
import jax.numpy as jnp
from jax import lax
from jax.experimental import pallas as pl
from jax.experimental.pallas import tpu as pltpu
from jax.sharding import Mesh
from jax.sharding import PartitionSpec as P

D = 4096
CAP = 8
LANES = 128
VMEM_LIMIT = 32 * 1024 * 1024
WIDE_LIMIT = 50 * 1024 * 1024
BF = jnp.bfloat16
F32 = jnp.float32
GROUP = ("y", "expert")


def ring(size, step):
    return [(i, (i + step) % size) for i in range(size)]


def whole(shape):
    return pl.BlockSpec(shape, lambda *_: (0,) * len(shape))


def attention(queries, keys, values, image_start):
    tok_rows, head_size = keys.shape
    heads_here = queries.shape[1] // head_size
    blocks = lax.axis_size("expert")
    query_pos = lax.axis_index("expert") * tok_rows + jnp.arange(tok_rows, dtype=jnp.int32)
    starts = image_start[0]
    inside = (query_pos[:, None] >= starts[None, :]) & (
        query_pos[:, None] < starts[None, :] + tok_rows
    )
    ends = jnp.broadcast_to(starts[None, :] + tok_rows - 1, inside.shape)
    visible_end = jnp.max(jnp.where(inside, ends, query_pos[:, None]), axis=1)
    grouped = queries.reshape(tok_rows, heads_here, head_size)
    own = jnp.concatenate([keys, values], axis=1)
    copies = jnp.broadcast_to(own[None], (blocks,) + own.shape)
    both = lax.all_to_all(copies, "expert", split_axis=0, concat_axis=0, tiled=True)
    both = both.reshape(blocks * tok_rows, 2 * head_size)
    all_keys, all_values = both[:, :head_size], both[:, head_size:]
    scores = jnp.einsum("thd,nd->htn", grouped, all_keys, preferred_element_type=F32)
    scores = scores * (1.0 / math.sqrt(head_size))
    key_pos = jnp.arange(all_keys.shape[0], dtype=jnp.int32)
    visible = (key_pos[None, :] <= visible_end[:, None])[None]
    row_max = jnp.max(jnp.where(visible, scores, -1e30), axis=2, keepdims=True)
    weights = jnp.where(visible, jnp.exp(scores - row_max), 0.0)
    row_total = jnp.sum(weights, axis=2)
    summed = jnp.einsum("htn,nd->htd", weights.astype(BF), all_values, preferred_element_type=F32)
    result = summed / row_total[:, :, None]
    return jnp.transpose(result, (1, 0, 2)).reshape(tok_rows, heads_here * head_size).astype(BF)


def move(source, target, sem):
    copy = pltpu.make_async_copy(source, target, sem)
    copy.start()
    return copy


def gate_up_kernel(here, rows, gain, gate, up, *rest, size, waits):
    outs = rest[waits : waits + size]
    scaled, gate_held, up_held, sems = rest[waits + size :]
    count, feat = rows.shape
    hidden = gate.shape[1]
    block, slab = count // size, feat // size
    copies = []
    for source, target in ((gate, gate_held), (up, up_held)):
        for k in range(size):
            part = pl.ds(k * slab, slab)
            copies.append(move(source.at[part, :], target.at[part, :], sems.at[len(copies)]))

    lane = lax.broadcasted_iota(jnp.int32, (block, LANES), 1)
    for k in range(size):
        at = pl.multiple_of(lax.rem(here[0] + k, size) * block, block)
        wide = rows[pl.ds(at, block), :].astype(F32)
        squares = jnp.sum(wide * wide, axis=1, keepdims=True)
        high = squares.astype(BF).astype(F32)
        extra = jnp.where(lane == 0, high, jnp.where(lane == 1, squares - high, 0.0))
        outs[k][:, 2 * hidden :] = extra.astype(BF)
        scaled[k * block : (k + 1) * block, :] = (wide * gain[...].astype(F32)).astype(BF)

    def product(weight, low):
        part = jnp.dot(scaled[...], weight[...], preferred_element_type=F32).astype(BF)
        for k in range(size):
            outs[k][:, low : low + hidden] = part[k * block : (k + 1) * block, :]

    for copy in copies[:size]:
        copy.wait()
    product(gate_held, 0)
    for copy in copies[size:]:
        copy.wait()
    product(up_held, hidden)


def gate_up(here, rows, gain, gate, up, after):
    size = lax.axis_size("tensor")
    feat, hidden = gate.shape
    count = rows.shape[0]
    block = count // size
    width = 2 * hidden + LANES
    near, far = pl.BlockSpec(memory_space=pltpu.VMEM), pl.BlockSpec(memory_space=pl.ANY)
    return pl.pallas_call(
        functools.partial(gate_up_kernel, size=size, waits=len(after)),
        in_specs=[pl.BlockSpec(memory_space=pltpu.SMEM), near, near, far, far]
        + [pl.BlockSpec(memory_space=pl.ANY)] * len(after),
        out_specs=[near] * size,
        scratch_shapes=[
            pltpu.VMEM(rows.shape, BF),
            pltpu.VMEM(gate.shape, BF),
            pltpu.VMEM(up.shape, BF),
            pltpu.SemaphoreType.DMA((2 * size,)),
        ],
        out_shape=[jax.ShapeDtypeStruct((block, width), BF)] * size,
        compiler_params=pltpu.CompilerParams(vmem_limit_bytes=WIDE_LIMIT),
        cost_estimate=pl.CostEstimate(
            flops=4 * count * feat * hidden,
            bytes_accessed=2 * (rows.size + 2 * gate.size + count * width),
            transcendentals=0,
        ),
    )(here, rows, gain, gate, up, *after)


def down_kernel(here, *refs, size, waits):
    pieces, down = refs[:size], refs[size]
    made, hidden = refs[size + 1 + waits], refs[size + 2 + waits]
    block = pieces[0].shape[0]

    @pl.when(pl.program_id(0) == 0)
    def _():
        for k in range(size):
            at = lax.rem(here[0] + size - k, size) * block
            hidden[pl.ds(pl.multiple_of(at, block), block), :] = pieces[k][...]

    made[...] = jnp.dot(hidden[...], down[...], preferred_element_type=F32).astype(BF)


def down_product(here, pieces, down, after):
    size = len(pieces)
    block, hidden = pieces[0].shape
    feat = down.shape[1]
    half = feat // 2
    rows = size * block
    return pl.pallas_call(
        functools.partial(down_kernel, size=size, waits=len(after)),
        grid_spec=pltpu.PrefetchScalarGridSpec(
            num_scalar_prefetch=1,
            grid=(2,),
            in_specs=[whole((block, hidden))] * size
            + [pl.BlockSpec((hidden, half), lambda i, _: (0, i))]
            + [pl.BlockSpec(memory_space=pl.ANY)] * len(after),
            out_specs=pl.BlockSpec((rows, half), lambda i, _: (0, i)),
            scratch_shapes=[pltpu.VMEM((rows, hidden), BF)],
        ),
        out_shape=jax.ShapeDtypeStruct((rows, feat), BF),
        compiler_params=pltpu.CompilerParams(vmem_limit_bytes=VMEM_LIMIT),
        cost_estimate=pl.CostEstimate(
            flops=2 * rows * hidden * feat,
            bytes_accessed=2 * (rows * hidden + hidden * feat + rows * feat),
            transcendentals=0,
        ),
    )(here, *pieces, down, *after)


def silu_product(parts, hidden):
    total = parts[0].astype(F32)
    for part in parts[1:]:
        total = total + part.astype(F32)
    squares = total[:, 2 * hidden : 2 * hidden + 1] + total[:, 2 * hidden + 1 : 2 * hidden + 2]
    scale = lax.rsqrt(squares / D + 1e-06)
    gate_sum = total[:, :hidden] * scale
    up_sum = total[:, hidden : 2 * hidden] * scale
    return (jax.nn.silu(gate_sum) * up_sum).astype(BF)


def silu_kernel(*refs):
    parts, out = refs[:-1], refs[-1]
    hidden = out.shape[1]

    def total(low, width):
        result = parts[0][:, low : low + width].astype(F32)
        for part in parts[1:]:
            result = result + part[:, low : low + width].astype(F32)
        return result

    extra = total(2 * hidden, LANES)
    scale = lax.rsqrt((extra[:, :1] + extra[:, 1:2]) / D + 1e-06)
    gate_sum = total(0, hidden) * scale
    up_sum = total(hidden, hidden) * scale
    out[...] = (gate_sum / (1.0 + jnp.exp(-gate_sum)) * up_sum).astype(BF)


def silu_call(parts, hidden):
    rows = parts[0].shape[0]
    near = pl.BlockSpec(memory_space=pltpu.VMEM)
    return pl.pallas_call(
        silu_kernel,
        in_specs=[near] * len(parts),
        out_specs=near,
        out_shape=jax.ShapeDtypeStruct((rows, hidden), BF),
        compiler_params=pltpu.CompilerParams(vmem_limit_bytes=VMEM_LIMIT),
        cost_estimate=pl.CostEstimate(
            flops=16 * rows * hidden,
            bytes_accessed=2 * rows * hidden * (2 * len(parts) + 1),
            transcendentals=rows * hidden,
        ),
    )(*parts)


def exchange(block):
    return lax.all_to_all(block, GROUP, split_axis=0, concat_axis=0, tiled=True)


def swap(block):
    return lax.ppermute(block, "core", [(0, 1), (1, 0)])


def per_device(
    queries,
    keys,
    values,
    image_start,
    norm_gain,
    expert_ids,
    gate_values,
    gate_weight,
    up_weight,
    down_weight,
):
    tok_rows, feat = queries.shape
    hidden_size = gate_weight.shape[2]
    size = lax.axis_size("tensor")
    zs = lax.axis_size("expert")
    peers = lax.axis_size("y") * zs
    rows = peers * CAP
    core = lax.axis_index("core")
    here = lax.axis_index("tensor").astype(jnp.int32)[None]
    gain = norm_gain[None]
    gate_rows, up_rows, down_rows = gate_weight[0], up_weight[0], down_weight[0]

    token = jnp.arange(tok_rows, dtype=jnp.int32)
    earlier = (token[:, None] < token[None, :]).astype(BF)
    level = jnp.arange(CAP, dtype=jnp.int32)[None, :, None]
    peer = jnp.arange(peers, dtype=jnp.int32)

    def plan(side):
        experts = (peer // zs * 2 + side) * zs + peer % zs
        named = expert_ids.T[:, None, :] == experts[None, :, None]
        member = jnp.any(named, axis=0)
        gate_of = jnp.sum(jnp.where(named, gate_values.T[:, None, :], 0.0), axis=0)
        rank = jnp.dot(member.astype(BF), earlier, preferred_element_type=F32)
        place = jnp.where(member, rank.astype(jnp.int32), -1)
        hit = place[:, None, :] == level
        high = lax.reduce_precision(gate_of, 8, 7)
        gates = jnp.concatenate([high, gate_of - high], axis=1)
        mix = jnp.where(jnp.concatenate([hit, hit], axis=2), gates[:, None, :], 0.0)
        pick = hit.astype(BF).reshape(rows, tok_rows)
        return pick, mix.astype(BF).reshape(rows, 2 * tok_rows)

    pick_near, mix_near = plan(core)
    pick_far, mix_far = plan(1 - core)
    attended = attention(queries, keys, values, image_start)

    def outgoing(pick):
        return jnp.dot(pick, attended, preferred_element_type=F32).astype(BF)

    def blocks(flat):
        return flat.reshape(peers, CAP, feat)

    steps = sorted(range(1, size), key=lambda step: -min(step, size - step))

    def fetch_parts(parts):
        got = {step: lax.ppermute(parts[step], "tensor", ring(size, step)) for step in steps}
        return [parts[0]] + [got[step] for step in range(1, size)]

    def spread(piece):
        return fetch_parts([piece] * size)

    def combine(mix, returned):
        both = lax.dot_general(
            mix,
            returned.reshape(rows, feat),
            (((0,), (0,)), ((), ())),
            preferred_element_type=F32,
        )
        return both[:tok_rows] + both[tok_rows:]

    near = exchange(blocks(outgoing(pick_near))).reshape(rows, feat)
    far = exchange(blocks(swap(outgoing(pick_far)))).reshape(rows, feat)

    near_parts = gate_up(here, near, gain, gate_rows, up_rows, [])
    near_got = fetch_parts(near_parts)
    early = near_got[0].astype(F32) + near_got.pop(size // 2).astype(F32)
    near_pieces = spread(silu_call([early] + near_got[1:], hidden_size))
    far_parts = list(gate_up(here, far, gain, gate_rows, up_rows, [near_pieces[0]]))
    for step in steps:
        near_pieces[step], far_parts[step] = lax.optimization_barrier(
            (near_pieces[step], far_parts[step])
        )
    near_made = down_product(here, near_pieces, down_rows, [far_parts[0]])
    far_got = fetch_parts(far_parts)
    near_back = exchange(blocks(near_made))
    far_hidden = silu_product(far_got, hidden_size)
    far_hidden = lax.all_gather(far_hidden, "tensor", axis=0, tiled=True)
    far_made = down_product(here, [far_hidden], down_rows, [])
    far_back = exchange(blocks(swap(far_made)))

    mixed = attended.astype(F32) + combine(mix_near, near_back) + combine(mix_far, far_back)
    return mixed.astype(BF)


def solution(mesh):
    dp, expert, tensor = mesh.devices.shape
    split = Mesh(
        mesh.devices.reshape(dp // 2, 2, expert, tensor), ("y", "core", "expert", "tensor")
    )
    both = ("y", "core", "expert")
    return jax.shard_map(
        per_device,
        mesh=split,
        in_specs=(
            P(both, "tensor"),
            P(both, "tensor"),
            P(both, "tensor"),
            P(("y", "core"), None),
            P("tensor"),
            P(both, None),
            P(both, None),
            P(both, "tensor", None),
            P(both, "tensor", None),
            P(both, None, "tensor"),
        ),
        out_specs=P(both, "tensor"),
        check_vma=False,
    )
```

```python
import functools
import math

import jax
import jax.numpy as jnp
from jax import lax
from jax.experimental import pallas as pl
from jax.experimental.pallas import tpu as pltpu
from jax.sharding import Mesh
from jax.sharding import PartitionSpec as P

D = 4096
CAP = 8
LANES = 128
VMEM_LIMIT = 32 * 1024 * 1024
WIDE_LIMIT = 50 * 1024 * 1024
BF = jnp.bfloat16
F32 = jnp.float32
GROUP = ("y", "expert")


def ring(size, step):
    return [(i, (i + step) % size) for i in range(size)]


def whole(shape):
    return pl.BlockSpec(shape, lambda *_: (0,) * len(shape))


def attention(queries, keys, values, image_start):
    tok_rows, head_size = keys.shape
    heads_here = queries.shape[1] // head_size
    blocks = lax.axis_size("expert")
    query_pos = lax.axis_index("expert") * tok_rows + jnp.arange(tok_rows, dtype=jnp.int32)
    starts = image_start[0]
    inside = (query_pos[:, None] >= starts[None, :]) & (
        query_pos[:, None] < starts[None, :] + tok_rows
    )
    ends = jnp.broadcast_to(starts[None, :] + tok_rows - 1, inside.shape)
    visible_end = jnp.max(jnp.where(inside, ends, query_pos[:, None]), axis=1)
    grouped = queries.reshape(tok_rows, heads_here, head_size)
    own = jnp.concatenate([keys, values], axis=1)
    copies = jnp.broadcast_to(own[None], (blocks,) + own.shape)
    both = lax.all_to_all(copies, "expert", split_axis=0, concat_axis=0, tiled=True)
    both = both.reshape(blocks * tok_rows, 2 * head_size)
    all_keys, all_values = both[:, :head_size], both[:, head_size:]
    scores = jnp.einsum("thd,nd->htn", grouped, all_keys, preferred_element_type=F32)
    scores = scores * (1.0 / math.sqrt(head_size))
    key_pos = jnp.arange(all_keys.shape[0], dtype=jnp.int32)
    visible = (key_pos[None, :] <= visible_end[:, None])[None]
    row_max = jnp.max(jnp.where(visible, scores, -1e30), axis=2, keepdims=True)
    weights = jnp.where(visible, jnp.exp(scores - row_max), 0.0)
    row_total = jnp.sum(weights, axis=2)
    summed = jnp.einsum("htn,nd->htd", weights.astype(BF), all_values, preferred_element_type=F32)
    result = summed / row_total[:, :, None]
    return jnp.transpose(result, (1, 0, 2)).reshape(tok_rows, heads_here * head_size).astype(BF)


def move(source, target, sem):
    copy = pltpu.make_async_copy(source, target, sem)
    copy.start()
    return copy


def gate_up_kernel(here, rows, gain, gate, up, *rest, size, waits):
    outs = rest[waits : waits + size]
    scaled, gate_held, up_held, sems = rest[waits + size :]
    count, feat = rows.shape
    hidden = gate.shape[1]
    block, slab = count // size, feat // size
    copies = []
    for source, target in ((gate, gate_held), (up, up_held)):
        for k in range(size):
            part = pl.ds(k * slab, slab)
            copies.append(move(source.at[part, :], target.at[part, :], sems.at[len(copies)]))

    lane = lax.broadcasted_iota(jnp.int32, (block, LANES), 1)
    for k in range(size):
        at = pl.multiple_of(lax.rem(here[0] + k, size) * block, block)
        wide = rows[pl.ds(at, block), :].astype(F32)
        squares = jnp.sum(wide * wide, axis=1, keepdims=True)
        high = squares.astype(BF).astype(F32)
        extra = jnp.where(lane == 0, high, jnp.where(lane == 1, squares - high, 0.0))
        outs[k][:, 2 * hidden :] = extra.astype(BF)
        scaled[k * block : (k + 1) * block, :] = (wide * gain[...].astype(F32)).astype(BF)

    def product(weight, low):
        part = jnp.dot(scaled[...], weight[...], preferred_element_type=F32).astype(BF)
        for k in range(size):
            outs[k][:, low : low + hidden] = part[k * block : (k + 1) * block, :]

    for copy in copies[:size]:
        copy.wait()
    product(gate_held, 0)
    for copy in copies[size:]:
        copy.wait()
    product(up_held, hidden)


def gate_up(here, rows, gain, gate, up, after):
    size = lax.axis_size("tensor")
    feat, hidden = gate.shape
    count = rows.shape[0]
    block = count // size
    width = 2 * hidden + LANES
    near, far = pl.BlockSpec(memory_space=pltpu.VMEM), pl.BlockSpec(memory_space=pl.ANY)
    return pl.pallas_call(
        functools.partial(gate_up_kernel, size=size, waits=len(after)),
        in_specs=[pl.BlockSpec(memory_space=pltpu.SMEM), near, near, far, far]
        + [pl.BlockSpec(memory_space=pl.ANY)] * len(after),
        out_specs=[near] * size,
        scratch_shapes=[
            pltpu.VMEM(rows.shape, BF),
            pltpu.VMEM(gate.shape, BF),
            pltpu.VMEM(up.shape, BF),
            pltpu.SemaphoreType.DMA((2 * size,)),
        ],
        out_shape=[jax.ShapeDtypeStruct((block, width), BF)] * size,
        compiler_params=pltpu.CompilerParams(vmem_limit_bytes=WIDE_LIMIT),
        cost_estimate=pl.CostEstimate(
            flops=4 * count * feat * hidden,
            bytes_accessed=2 * (rows.size + 2 * gate.size + count * width),
            transcendentals=0,
        ),
    )(here, rows, gain, gate, up, *after)


def down_kernel(here, *refs, size, waits):
    pieces, down = refs[:size], refs[size]
    made, hidden = refs[size + 1 + waits], refs[size + 2 + waits]
    block = pieces[0].shape[0]

    @pl.when(pl.program_id(0) == 0)
    def _():
        for k in range(size):
            at = lax.rem(here[0] + size - k, size) * block
            hidden[pl.ds(pl.multiple_of(at, block), block), :] = pieces[k][...]

    made[...] = jnp.dot(hidden[...], down[...], preferred_element_type=F32).astype(BF)


def down_product(here, pieces, down, after):
    size = len(pieces)
    block, hidden = pieces[0].shape
    feat = down.shape[1]
    half = feat // 2
    rows = size * block
    return pl.pallas_call(
        functools.partial(down_kernel, size=size, waits=len(after)),
        grid_spec=pltpu.PrefetchScalarGridSpec(
            num_scalar_prefetch=1,
            grid=(2,),
            in_specs=[whole((block, hidden))] * size
            + [pl.BlockSpec((hidden, half), lambda i, _: (0, i))]
            + [pl.BlockSpec(memory_space=pl.ANY)] * len(after),
            out_specs=pl.BlockSpec((rows, half), lambda i, _: (0, i)),
            scratch_shapes=[pltpu.VMEM((rows, hidden), BF)],
        ),
        out_shape=jax.ShapeDtypeStruct((rows, feat), BF),
        compiler_params=pltpu.CompilerParams(vmem_limit_bytes=VMEM_LIMIT),
        cost_estimate=pl.CostEstimate(
            flops=2 * rows * hidden * feat,
            bytes_accessed=2 * (rows * hidden + hidden * feat + rows * feat),
            transcendentals=0,
        ),
    )(here, *pieces, down, *after)


def silu_product(parts, hidden):
    total = parts[0].astype(F32)
    for part in parts[1:]:
        total = total + part.astype(F32)
    squares = total[:, 2 * hidden : 2 * hidden + 1] + total[:, 2 * hidden + 1 : 2 * hidden + 2]
    scale = lax.rsqrt(squares / D + 1e-06)
    gate_sum = total[:, :hidden] * scale
    up_sum = total[:, hidden : 2 * hidden] * scale
    return (jax.nn.silu(gate_sum) * up_sum).astype(BF)


def silu_kernel(*refs):
    parts, out = refs[:-1], refs[-1]
    hidden = out.shape[1]

    def total(low, width):
        result = parts[0][:, low : low + width].astype(F32)
        for part in parts[1:]:
            result = result + part[:, low : low + width].astype(F32)
        return result

    extra = total(2 * hidden, LANES)
    scale = lax.rsqrt((extra[:, :1] + extra[:, 1:2]) / D + 1e-06)
    gate_sum = total(0, hidden) * scale
    up_sum = total(hidden, hidden) * scale
    out[...] = (gate_sum / (1.0 + jnp.exp(-gate_sum)) * up_sum).astype(BF)


def silu_call(parts, hidden):
    rows = parts[0].shape[0]
    near = pl.BlockSpec(memory_space=pltpu.VMEM)
    return pl.pallas_call(
        silu_kernel,
        in_specs=[near] * len(parts),
        out_specs=near,
        out_shape=jax.ShapeDtypeStruct((rows, hidden), BF),
        compiler_params=pltpu.CompilerParams(vmem_limit_bytes=VMEM_LIMIT),
        cost_estimate=pl.CostEstimate(
            flops=16 * rows * hidden,
            bytes_accessed=2 * rows * hidden * (2 * len(parts) + 1),
            transcendentals=rows * hidden,
        ),
    )(*parts)


def exchange(block):
    return lax.all_to_all(block, GROUP, split_axis=0, concat_axis=0, tiled=True)


def swap(block):
    return lax.ppermute(block, "core", [(0, 1), (1, 0)])


def per_device(
    queries,
    keys,
    values,
    image_start,
    norm_gain,
    expert_ids,
    gate_values,
    gate_weight,
    up_weight,
    down_weight,
):
    tok_rows, feat = queries.shape
    hidden_size = gate_weight.shape[2]
    size = lax.axis_size("tensor")
    zs = lax.axis_size("expert")
    peers = lax.axis_size("y") * zs
    rows = peers * CAP
    core = lax.axis_index("core")
    here = lax.axis_index("tensor").astype(jnp.int32)[None]
    gain = norm_gain[None]
    gate_rows, up_rows, down_rows = gate_weight[0], up_weight[0], down_weight[0]

    token = jnp.arange(tok_rows, dtype=jnp.int32)
    earlier = (token[:, None] < token[None, :]).astype(BF)
    level = jnp.arange(CAP, dtype=jnp.int32)[None, :, None]
    peer = jnp.arange(peers, dtype=jnp.int32)

    def plan(side):
        experts = (peer // zs * 2 + side) * zs + peer % zs
        named = expert_ids.T[:, None, :] == experts[None, :, None]
        member = jnp.any(named, axis=0)
        gate_of = jnp.sum(jnp.where(named, gate_values.T[:, None, :], 0.0), axis=0)
        rank = jnp.dot(member.astype(BF), earlier, preferred_element_type=F32)
        place = jnp.where(member, rank.astype(jnp.int32), -1)
        hit = place[:, None, :] == level
        high = lax.reduce_precision(gate_of, 8, 7)
        gates = jnp.concatenate([high, gate_of - high], axis=1)
        mix = jnp.where(jnp.concatenate([hit, hit], axis=2), gates[:, None, :], 0.0)
        pick = hit.astype(BF).reshape(rows, tok_rows)
        return pick, mix.astype(BF).reshape(rows, 2 * tok_rows)

    pick_near, mix_near = plan(core)
    pick_far, mix_far = plan(1 - core)
    attended = attention(queries, keys, values, image_start)

    def outgoing(pick):
        return jnp.dot(pick, attended, preferred_element_type=F32).astype(BF)

    def blocks(flat):
        return flat.reshape(peers, CAP, feat)

    steps = sorted(range(1, size), key=lambda step: -min(step, size - step))

    def fetch_parts(parts):
        got = {step: lax.ppermute(parts[step], "tensor", ring(size, step)) for step in steps}
        return [parts[0]] + [got[step] for step in range(1, size)]

    def spread(piece):
        return fetch_parts([piece] * size)

    def combine(mix, returned):
        both = lax.dot_general(
            mix,
            returned.reshape(rows, feat),
            (((0,), (0,)), ((), ())),
            preferred_element_type=F32,
        )
        return both[:tok_rows] + both[tok_rows:]

    near = exchange(blocks(outgoing(pick_near))).reshape(rows, feat)
    far = exchange(blocks(swap(outgoing(pick_far)))).reshape(rows, feat)

    near_parts = gate_up(here, near, gain, gate_rows, up_rows, [])
    near_got = fetch_parts(near_parts)
    early = near_got[0].astype(F32) + near_got.pop(size // 2).astype(F32)
    near_pieces = spread(silu_call([early] + near_got[1:], hidden_size))
    far_parts = list(gate_up(here, far, gain, gate_rows, up_rows, [near_pieces[0]]))
    for step in steps:
        near_pieces[step], far_parts[step] = lax.optimization_barrier(
            (near_pieces[step], far_parts[step])
        )
    near_made = down_product(here, near_pieces, down_rows, [far_parts[0]])
    far_got = fetch_parts(far_parts)
    far_got = [far_got[0].astype(F32) + far_got.pop(size // 2).astype(F32)] + far_got[1:]
    near_back = exchange(blocks(near_made))
    far_hidden = silu_product(far_got, hidden_size)
    far_hidden = lax.all_gather(far_hidden, "tensor", axis=0, tiled=True)
    far_made = down_product(here, [far_hidden], down_rows, [])
    far_back = exchange(blocks(swap(far_made)))

    mixed = attended.astype(F32) + combine(mix_near, near_back) + combine(mix_far, far_back)
    return mixed.astype(BF)


def solution(mesh):
    dp, expert, tensor = mesh.devices.shape
    split = Mesh(
        mesh.devices.reshape(dp // 2, 2, expert, tensor), ("y", "core", "expert", "tensor")
    )
    both = ("y", "core", "expert")
    return jax.shard_map(
        per_device,
        mesh=split,
        in_specs=(
            P(both, "tensor"),
            P(both, "tensor"),
            P(both, "tensor"),
            P(("y", "core"), None),
            P("tensor"),
            P(both, None),
            P(both, None),
            P(both, "tensor", None),
            P(both, "tensor", None),
            P(both, None, "tensor"),
        ),
        out_specs=P(both, "tensor"),
        check_vma=False,
    )
```
